32 devices in a mesh: ctx: 4 (over y, core), grp: 8 (over z, x).
Axes of the slice: x: 2, y: 2, z: 4, core: 2. Of those that a mesh axis runs over, the one named last changes fastest.
Arguments:
- tokens: bfloat16 [4096, 4096], P(('ctx', 'grp')), may hold values from -6 to 6
- cotangent: bfloat16 [4096, 4096], P(('ctx', 'grp')), may hold values from -6 to 6
- conv_weight: float32 [3, 7, 4096], P(None, None, 'grp'), may hold values from -2 to 2
- residue: float32 [16, 4096], P(None, 'grp'), may hold values from -1.5 to 1.5
- decay_length: float32 [16, 4096], P(None, 'grp'), may hold values from 3 to 81920, as said below
- skip_gain: float32 [4096], P('grp'), may hold values from 0.5 to 1.5
Outputs:
- grad_tokens: bfloat16 [4096, 4096], P('ctx', 'grp')
The draws below stay inside these ranges and needn't reach their ends.
Inputs may be any that keep to these rules, and one draw needn't show every extreme that they name: `decay_length`: each entry is a decay length in tokens.
All inputs are finite; a program needn't handle non-finite values.
Results may differ from the reference program's by a relative error of at most 0.001.
Values may be sent and summed in bfloat16 or wider, within the bound.
A program may use at most 128 MiB of HBM per device.

```python
import jax
import jax.numpy as jnp
from jax import lax

DW = 4096
POLES = 16
KW = 7
TOKENS = 4096


def draw_decay_length(key, part):
    slow_key, spread_key = jax.random.split(key)
    slow_share = 0.5
    slow_mask = jax.random.uniform(slow_key, (POLES, DW), dtype=jnp.float32) < slow_share
    spread = jax.random.uniform(spread_key, (POLES, DW), dtype=jnp.float32)
    slow_len = jnp.exp(jnp.log(0.5 * TOKENS) + spread * jnp.log(40.0))
    fast_len = jnp.exp(jnp.log(3.0) + spread * jnp.log(50.0 / 3.0))
    return jnp.where(slow_mask, slow_len, fast_len).astype(jnp.float32)


def block_levels(stream_key, dims, pieces, smallest, high):
    level, own = 1.0, jax.random.fold_in(stream_key, 6)
    for position, shards_of in pieces:
        steps = jnp.exp(jax.random.uniform(jax.random.fold_in(own, position), (shards_of,), jnp.float32, smallest / len(pieces), high / len(pieces)))
        level = level * jnp.repeat(steps, dims[position] // shards_of).reshape([-1 if axis == position else 1 for axis in range(len(dims))])
    return level


def gaussian(key, dims, scale, limit, pieces=(), kind=jnp.bfloat16):
    values = scale * jax.random.normal(key, dims, jnp.float32)
    if pieces:
        values = values * block_levels(key, dims, pieces, -0.22, 0.18)
    return jnp.clip(values, -limit, limit).astype(kind)


def setup_inputs(seed: int = 0) -> dict:
    key_list = jax.random.split(jax.random.key(seed), 7)
    tokens = gaussian(key_list[0], (TOKENS, DW), 1.0, 6.0, ((0, 32),))
    cotangent = gaussian(key_list[1], (TOKENS, DW), 1.0, 6.0, ((0, 32),))
    conv_weight = gaussian(key_list[2], (3, KW, DW), KW ** -0.5, 2.0, ((2, 8),), jnp.float32)
    residue = gaussian(key_list[3], (POLES, DW), 0.25, 1.5, ((1, 8),), jnp.float32)
    decay_length = draw_decay_length(jax.random.fold_in(key_list[6], 71), 0)
    skip_gain = jnp.clip(0.5 + 1.0 * jax.random.uniform(key_list[5], (DW,), jnp.float32) ** block_levels(key_list[5], (DW,), ((0, 8),), -0.2, 0.2), 0.5, 1.5)
    return {"tokens": tokens, "cotangent": cotangent, "conv_weight": conv_weight, "residue": residue, "decay_length": decay_length, "skip_gain": skip_gain}


def channel_group(operands):
    inputs, grad_in, filters, residue, lengths, skip_gain = operands
    tap_count = filters.shape[1]
    seq_len = inputs.shape[0]
    padded = jnp.pad(inputs.astype(jnp.float32), ((tap_count - 1, 0), (0, 0)))
    filtered = sum((filters[:, offset][:, None, :] * padded[None, tap_count - 1 - offset:tap_count - 1 - offset + seq_len] for offset in range(tap_count)))
    queries, key_rows, value_rows = (filtered[0], filtered[1], filtered[2])
    source = key_rows * value_rows
    inverse = 1.0 / lengths
    forget = -jnp.expm1(-inverse)
    modal_gain = residue * jnp.sqrt(-jnp.expm1(-2.0 * inverse))

    def advance(carried, current):
        carried = carried - forget * carried + current
        return (carried, lax.optimization_barrier(jnp.sum(modal_gain * carried, 0)))
    start_state = jnp.zeros(residue.shape, jnp.float32)
    final_state, mixed_sum = lax.scan(advance, start_state, source)
    long_out = mixed_sum + skip_gain * source
    grad_out = grad_in.astype(jnp.float32)
    d_long = grad_out * queries
    d_queries = grad_out * long_out
    final_adjoint, back_sum = lax.scan(advance, start_state, d_long, reverse=True)
    d_source = back_sum + skip_gain * d_long
    d_filtered = jnp.stack([d_queries, d_source * value_rows, d_source * key_rows])
    trailing = jnp.pad(d_filtered, ((0, 0), (0, tap_count - 1), (0, 0)))
    grad_rows = sum((lax.optimization_barrier(jnp.sum(filters[:, offset][:, None, :] * trailing[:, offset:offset + seq_len], 0)) for offset in range(tap_count)))
    return grad_rows.astype(jnp.bfloat16)

def reference(tokens, cotangent, conv_weight, residue, decay_length, skip_gain):
    group_width = min(256, DW)
    groups = DW // group_width

    def by_group(array):
        return jnp.moveaxis(array.reshape(array.shape[:-1] + (groups, group_width)), -2, 0)
    results = lax.map(channel_group, (by_group(tokens), by_group(cotangent), by_group(conv_weight), by_group(residue), by_group(decay_length), by_group(skip_gain)))
    return jnp.moveaxis(results, 0, 1).reshape(TOKENS, DW)
```

```python
import functools

import jax
import jax.numpy as jnp
from jax import lax
from jax.experimental import pallas as pl
from jax.experimental.pallas import tpu as pltpu
from jax.sharding import PartitionSpec as P

LANES = 128
SEGS = 8
HALO = 16


def repeat(count, unroll, body, carry):
    whole = count // unroll

    def group(index, carried):
        for step in range(unroll):
            carried = body(index * unroll + step, carried)
        return carried

    carry = lax.fori_loop(0, whole, group, carry)
    for step in range(whole * unroll, count):
        carry = body(step, carry)
    return carry


def tree_sum(terms):
    terms = list(terms)
    while len(terms) > 1:
        terms = [
            terms[i] + terms[i + 1] if i + 1 < len(terms) else terms[i]
            for i in range(0, len(terms), 2)
        ]
    return terms[0]


def spread(row):
    return jnp.broadcast_to(row, (SEGS, LANES))


def relayout(natural, turned, first, count, length):
    def body(j, _):
        turned[j] = natural[pl.ds(first + j, SEGS, stride=length), :]
        return 0

    repeat(count, 8, body, 0)


def convolve(length, taps, w_ref, xt, ct, q_at, k_at, v_at, src, ups):
    weights = [[spread(w_ref[k, i : i + 1, :]) for i in range(taps)] for k in range(3)]

    def body(t, _):
        window = [xt[t + taps - 1 - i] for i in range(taps)]
        q, k, v = (tree_sum(weights[s][i] * window[i] for i in range(taps)) for s in range(3))
        if q_at is not None:
            q_at[t] = q
        if k_at is not None:
            k_at[t] = k
            v_at[t] = v
        src[t] = k * v
        ups[t] = q * ct[t]
        return 0

    repeat(length, 3, body, 0)


def local_states(length, poles, decay, src, ups, ends, heads):
    d = [spread(decay[p : p + 1, :]) for p in range(poles)]
    zero = jnp.zeros((SEGS, LANES), jnp.float32)

    def body(t, states):
        x, u = src[t], ups[length - 1 - t]
        return (
            tuple(d[p] * states[0][p] + x for p in range(poles)),
            tuple(d[p] * states[1][p] + u for p in range(poles)),
        )

    states = ((zero,) * poles, (zero,) * poles)
    short = length - SEGS
    states = repeat(short, 4, body, states)
    for p in range(poles):
        ends[1, p * SEGS : (p + 1) * SEGS, :] = states[0][p]
        heads[1, p * SEGS : (p + 1) * SEGS, :] = states[1][p]
    for t in range(SEGS):
        states = body(short + t, states)
    for p in range(poles):
        ends[0, p * SEGS : (p + 1) * SEGS, :] = states[0][p]
        heads[0, p * SEGS : (p + 1) * SEGS, :] = states[1][p]


def link_segments(length, poles, inverse, ends, heads, starts, nexts):
    over = jnp.exp(-float(length) * inverse)
    partial = jnp.exp(-float(length - SEGS) * inverse)
    carried = jnp.zeros_like(inverse)
    for s in range(SEGS):
        starts[s] = carried
        if s < SEGS - 1:
            carried = over * carried + ends[0, pl.ds(s, poles, stride=SEGS), :]
    total = partial * carried + ends[1, pl.ds(SEGS - 1, poles, stride=SEGS), :]
    carried = jnp.zeros_like(inverse)
    for s in reversed(range(SEGS)):
        nexts[s] = carried
        if s:
            carried = over * carried + heads[0, pl.ds(s, poles, stride=SEGS), :]
    return total, partial * carried + heads[1, pl.ds(0, poles, stride=SEGS), :]


def enter(length, poles, inverse, incoming, after, starts, nexts, begin, finish):
    for s in range(SEGS):
        begin[pl.ds(s, poles, stride=SEGS), :] = (
            starts[s] + jnp.exp(-float(s * length) * inverse) * incoming
        )
        finish[pl.ds(s, poles, stride=SEGS), :] = (
            nexts[s] + jnp.exp(-float((SEGS - 1 - s) * length) * inverse) * after
        )


def mix(length, poles, backward, decay, gain, skip, entering, stream, store):
    d = [spread(decay[p : p + 1, :]) for p in range(poles)]
    g = [spread(gain[p : p + 1, :]) for p in range(poles)]
    skip = spread(skip)
    states = tuple(entering[p * SEGS : (p + 1) * SEGS, :] for p in range(poles))

    def body(step, states):
        t = length - 1 - step if backward else step
        x = stream[t]
        states = tuple(d[p] * states[p] + x for p in range(poles))
        store(t, tree_sum([g[p] * states[p] for p in range(poles)] + [skip * x]))
        return states

    repeat(length, 4, body, states)


def gather_taps(length, taps, w_ref, streams, natural):
    weights = [[spread(w_ref[k, i : i + 1, :]) for i in range(taps)] for k in range(3)]
    for stream in streams:
        for j in range(taps - 1):
            stream[length + j] = pltpu.roll(stream[j], SEGS - 1, 0)

    def body(t, _):
        grad = tree_sum(
            tree_sum(weights[k][i] * streams[k][t + i] for i in range(taps)) for k in range(3)
        )
        natural[pl.ds(t, SEGS, stride=length), :] = grad
        return 0

    repeat(length, 3, body, 0)


def stage(rows, taps, before, tok, after, cot, cot_after, natural, cnat, xt, ct):
    length = rows // SEGS + 1
    natural[0:HALO, :] = before[...].astype(jnp.float32)
    natural[HALO : HALO + rows, :] = tok[...].astype(jnp.float32)
    natural[HALO + rows : HALO + rows + HALO, :] = after[...].astype(jnp.float32)
    cnat[0:rows, :] = cot[...].astype(jnp.float32)
    cnat[rows : rows + HALO, :] = cot_after[...].astype(jnp.float32)
    relayout(natural, xt, HALO - (taps - 1), length + taps - 1, length)
    relayout(cnat, ct, 0, length, length)


def first_kernel(rows, poles, taps, before, tok, after, cot, cot_after, w_ref, inv_ref,
                 starts, nexts, sums, natural, cnat, xt, ct, src, ups, decay, ends, heads):
    length = rows // SEGS + 1
    stage(rows, taps, before, tok, after, cot, cot_after, natural, cnat, xt, ct)
    convolve(length, taps, w_ref, xt, ct, None, None, None, src, ups)
    inverse = inv_ref[...]
    decay[...] = jnp.exp(-inverse)
    local_states(length, poles, decay, src, ups, ends, heads)
    total, head = link_segments(length, poles, inverse, ends, heads, starts, nexts)
    sums[0] = total
    sums[1] = head


def second_kernel(rows, poles, taps, before, tok, after, cot, cot_after, w_ref, inv_ref, gain, skip,
                  starts, nexts, entry, out, natural, cnat, xt, ct, k_at, v_at, src, ups, dq,
                  decay, begin, finish):
    length = rows // SEGS + 1
    stage(rows, taps, before, tok, after, cot, cot_after, natural, cnat, xt, ct)
    convolve(length, taps, w_ref, xt, ct, None, k_at, v_at, src, ups)
    inverse = inv_ref[...]
    decay[...] = jnp.exp(-inverse)
    enter(length, poles, inverse, entry[0], entry[1], starts, nexts, begin, finish)

    def store_q(t, value):
        dq[t] = ct[t] * value

    def store_kv(t, value):
        k, v = k_at[t], v_at[t]
        k_at[t] = value * v
        v_at[t] = value * k

    mix(length, poles, False, decay, gain, skip[...], begin, src, store_q)
    mix(length, poles, True, decay, gain, skip[...], finish, ups, store_kv)
    gather_taps(length, taps, w_ref, (dq, k_at, v_at), natural)
    out[...] = natural[0:rows, :].astype(jnp.bfloat16)


def shifted(block, axis, distance):
    devices = range(lax.axis_size(axis))
    route = [(i - distance, i) for i in devices if i - distance in devices]
    return lax.ppermute(block, axis, route)


def per_device(tokens, cotangent, conv_weight, residue, decay_length, skip_gain):
    tok = lax.all_to_all(tokens, "grp", split_axis=1, concat_axis=0, tiled=True)
    cot = lax.all_to_all(cotangent, "grp", split_axis=1, concat_axis=0, tiled=True)
    rows, chans = tok.shape
    poles, taps = residue.shape[0], conv_weight.shape[1]
    length = rows // SEGS + 1
    inverse = 1.0 / decay_length
    gain = residue * jnp.sqrt(-jnp.expm1(-2.0 * inverse))
    before = shifted(tok[rows - HALO :], "ctx", 1)
    behind = shifted(jnp.concatenate([tok[:HALO], cot[:HALO]], 0), "ctx", -1)
    after, cot_after = behind[:HALO], behind[HALO:]
    f32 = jnp.float32

    def cols(*lead):
        return pl.BlockSpec((*lead, LANES), lambda c: (0,) * len(lead) + (c,))

    def shape(*dims):
        return jax.ShapeDtypeStruct(dims, f32)

    def turned(extra=0):
        return pltpu.VMEM((length + extra, SEGS, LANES), f32)

    grid = (chans // LANES,)
    edge, whole = cols(HALO), cols(rows)
    base = [edge, whole, edge, whole, edge, cols(3, taps), cols(poles)]
    data = (before, tok, after, cot, cot_after, conv_weight, inverse)
    params = pltpu.CompilerParams(vmem_limit_bytes=56 * 2**20)
    natural = pltpu.VMEM((rows + 2 * HALO, LANES), f32)
    small = pltpu.VMEM((poles * SEGS, LANES), f32)
    starts, nexts, sums = pl.pallas_call(
        functools.partial(first_kernel, rows, poles, taps),
        grid=grid,
        out_shape=(shape(SEGS, poles, chans), shape(SEGS, poles, chans), shape(2, poles, chans)),
        in_specs=base,
        out_specs=(cols(SEGS, poles), cols(SEGS, poles), cols(2, poles)),
        scratch_shapes=[
            natural, natural, turned(taps - 1), turned(), turned(), turned(),
            pltpu.VMEM((poles, LANES), f32),
            pltpu.VMEM((2, poles * SEGS, LANES), f32),
            pltpu.VMEM((2, poles * SEGS, LANES), f32),
        ],
        compiler_params=params,
    )(*data)
    every = lax.all_gather(sums, "ctx")
    me = lax.axis_index("ctx")
    over = jnp.exp(-float(rows) * inverse)
    incoming = jnp.zeros_like(inverse)
    later = jnp.zeros_like(inverse)
    for j in range(lax.axis_size("ctx")):
        incoming = jnp.where(j < me, over * incoming + every[j, 0], incoming)
        r = lax.axis_size("ctx") - 1 - j
        later = jnp.where(r > me, over * later + every[r, 1], later)
    entry = jnp.stack([incoming, later])
    return pl.pallas_call(
        functools.partial(second_kernel, rows, poles, taps),
        grid=grid,
        out_shape=jax.ShapeDtypeStruct((rows, chans), jnp.bfloat16),
        in_specs=base + [cols(poles), cols(1), cols(SEGS, poles), cols(SEGS, poles), cols(2, poles)],
        out_specs=whole,
        scratch_shapes=[
            natural, natural, turned(taps - 1), turned(),
            turned(taps - 1), turned(taps - 1), turned(), turned(), turned(taps - 1),
            pltpu.VMEM((poles, LANES), f32), small, small,
        ],
        compiler_params=params,
    )(*data, gain, skip_gain[None], starts, nexts, entry)


def solution(mesh):
    placed = (
        P(("ctx", "grp"), None),
        P(("ctx", "grp"), None),
        P(None, None, "grp"),
        P(None, "grp"),
        P(None, "grp"),
        P("grp"),
    )
    return jax.shard_map(
        per_device, mesh=mesh, in_specs=placed, out_specs=P("ctx", "grp"), check_vma=False
    )
```

```python
import functools

import jax
import jax.numpy as jnp
from jax import lax
from jax.experimental import pallas as pl
from jax.experimental.pallas import tpu as pltpu
from jax.sharding import PartitionSpec as P

MESH = pl.DeviceIdType.MESH
LANES = 128
SEGS = 8
HALO = 16


def repeat(count, unroll, body, carry):
    whole = count // unroll

    def group(index, carried):
        for step in range(unroll):
            carried = body(index * unroll + step, carried)
        return carried

    carry = lax.fori_loop(0, whole, group, carry)
    for step in range(whole * unroll, count):
        carry = body(step, carry)
    return carry


def tree_sum(terms):
    terms = list(terms)
    while len(terms) > 1:
        terms = [
            terms[i] + terms[i + 1] if i + 1 < len(terms) else terms[i]
            for i in range(0, len(terms), 2)
        ]
    return terms[0]


def spread(row):
    return jnp.broadcast_to(row, (SEGS, LANES))


def relayout(natural, turned, first, count, length):
    def body(j, _):
        turned[j] = natural[pl.ds(first + j, SEGS, stride=length), :]
        return 0

    repeat(count, 8, body, 0)


def convolve(length, taps, w_ref, xt, ct, q_at, k_at, v_at, src, ups):
    weights = [[spread(w_ref[k, i : i + 1, :]) for i in range(taps)] for k in range(3)]

    def body(t, _):
        window = [xt[t + taps - 1 - i] for i in range(taps)]
        q, k, v = (tree_sum(weights[s][i] * window[i] for i in range(taps)) for s in range(3))
        if q_at is not None:
            q_at[t] = q
        if k_at is not None:
            k_at[t] = k
            v_at[t] = v
        src[t] = k * v
        ups[t] = q * ct[t]
        return 0

    repeat(length, 3, body, 0)


def local_states(length, poles, decay, src, ups, ends, heads):
    d = [spread(decay[p : p + 1, :]) for p in range(poles)]
    zero = jnp.zeros((SEGS, LANES), jnp.float32)

    def body(t, states):
        x, u = src[t], ups[length - 1 - t]
        return (
            tuple(d[p] * states[0][p] + x for p in range(poles)),
            tuple(d[p] * states[1][p] + u for p in range(poles)),
        )

    states = ((zero,) * poles, (zero,) * poles)
    short = length - SEGS
    states = repeat(short, 4, body, states)
    for p in range(poles):
        ends[1, p * SEGS : (p + 1) * SEGS, :] = states[0][p]
        heads[1, p * SEGS : (p + 1) * SEGS, :] = states[1][p]
    for t in range(SEGS):
        states = body(short + t, states)
    for p in range(poles):
        ends[0, p * SEGS : (p + 1) * SEGS, :] = states[0][p]
        heads[0, p * SEGS : (p + 1) * SEGS, :] = states[1][p]


def link_segments(length, poles, inverse, ends, heads, starts, nexts):
    over = jnp.exp(-float(length) * inverse)
    partial = jnp.exp(-float(length - SEGS) * inverse)
    carried = jnp.zeros_like(inverse)
    for s in range(SEGS):
        starts[s] = carried
        if s < SEGS - 1:
            carried = over * carried + ends[0, pl.ds(s, poles, stride=SEGS), :]
    total = partial * carried + ends[1, pl.ds(SEGS - 1, poles, stride=SEGS), :]
    carried = jnp.zeros_like(inverse)
    for s in reversed(range(SEGS)):
        nexts[s] = carried
        if s:
            carried = over * carried + heads[0, pl.ds(s, poles, stride=SEGS), :]
    return total, partial * carried + heads[1, pl.ds(0, poles, stride=SEGS), :]


def enter(length, poles, inverse, incoming, after, starts, nexts, begin, finish):
    for s in range(SEGS):
        begin[pl.ds(s, poles, stride=SEGS), :] = (
            starts[s] + jnp.exp(-float(s * length) * inverse) * incoming
        )
        finish[pl.ds(s, poles, stride=SEGS), :] = (
            nexts[s] + jnp.exp(-float((SEGS - 1 - s) * length) * inverse) * after
        )


def mix(length, poles, backward, decay, gain, skip, entering, stream, store):
    d = [spread(decay[p : p + 1, :]) for p in range(poles)]
    g = [spread(gain[p : p + 1, :]) for p in range(poles)]
    skip = spread(skip)
    states = tuple(entering[p * SEGS : (p + 1) * SEGS, :] for p in range(poles))

    def body(step, states):
        t = length - 1 - step if backward else step
        x = stream[t]
        states = tuple(d[p] * states[p] + x for p in range(poles))
        store(t, tree_sum([g[p] * states[p] for p in range(poles)] + [skip * x]))
        return states

    repeat(length, 4, body, states)


def gather_taps(length, taps, w_ref, streams, natural):
    weights = [[spread(w_ref[k, i : i + 1, :]) for i in range(taps)] for k in range(3)]
    for stream in streams:
        for j in range(taps - 1):
            stream[length + j] = pltpu.roll(stream[j], SEGS - 1, 0)

    def body(t, _):
        grad = tree_sum(
            tree_sum(weights[k][i] * streams[k][t + i] for i in range(taps)) for k in range(3)
        )
        natural[pl.ds(t, SEGS, stride=length), :] = grad
        return 0

    repeat(length, 3, body, 0)


def stage(rows, taps, before, tok, after, cot, cot_after, natural, cnat, xt, ct):
    length = rows // SEGS + 1
    natural[0:HALO, :] = before.astype(jnp.float32)
    natural[HALO : HALO + rows, :] = tok.astype(jnp.float32)
    natural[HALO + rows : HALO + rows + HALO, :] = after.astype(jnp.float32)
    cnat[0:rows, :] = cot.astype(jnp.float32)
    cnat[rows : rows + HALO, :] = cot_after.astype(jnp.float32)
    relayout(natural, xt, HALO - (taps - 1), length + taps - 1, length)
    relayout(cnat, ct, 0, length, length)


def kernel(ctxs, grps, poles, taps, tokens, cotangent, w_ref, inv_ref, gain_ref, skip_ref, out,
           tok_in, cot_in, before, after, cot_after, every,
           natural, cnat, xt, ct, k_at, v_at, src, ups, dq,
           decay, weights, gain, ends, heads, starts, nexts, begin, finish,
           send_sem, recv_sem, edge_send, edge_recv, state_send, state_recv):
    ctx, grp = lax.axis_index("ctx"), lax.axis_index("grp")
    share, chans = tokens.shape[0], out.shape[1]
    rows = share * grps
    length = rows // SEGS + 1
    chunks = chans // LANES
    first, last = ctx == 0, ctx == ctxs - 1
    lead, tail = grp == 0, grp == grps - 1

    barrier = pltpu.get_barrier_semaphore()

    def greet(to_ctx, to_grp):
        pl.semaphore_signal(barrier, inc=1, device_id=(to_ctx, to_grp), device_id_type=MESH)

    for off in range(1, grps):
        greet(ctx, lax.rem(grp + off, grps))
    for off in range(1, ctxs):
        greet(lax.rem(ctx + off, ctxs), grp)

    @pl.when(ctx > 0)
    def _():
        greet(ctx - 1, grps - 1)

    @pl.when(ctx < ctxs - 1)
    def _():
        greet(ctx + 1, 0)

    sends_tail = jnp.logical_and(tail, ctx < ctxs - 1)
    sends_lead = jnp.logical_and(lead, ctx > 0)
    edges = jnp.where(sends_tail, grps, 0) + jnp.where(sends_lead, grps, 0)
    pl.semaphore_wait(barrier, grps - 1 + ctxs - 1 + edges)

    def edge_copy(kind, j):
        source = (tokens, tokens, cotangent)[kind]
        row = share - HALO if kind == 0 else 0
        return pltpu.make_async_remote_copy(
            src_ref=source.at[row : row + HALO, pl.ds(pl.multiple_of(j * chans, LANES), chans)],
            dst_ref=(before, after, cot_after)[kind],
            send_sem=edge_send.at[kind, j],
            recv_sem=edge_recv.at[kind],
            device_id=(ctx + 1 if kind == 0 else ctx - 1, j),
            device_id_type=MESH,
        )

    @pl.when(sends_tail)
    def _():
        for j in range(grps):
            edge_copy(0, j).start()

    @pl.when(sends_lead)
    def _():
        for j in range(grps):
            edge_copy(1, j).start()
            edge_copy(2, j).start()

    def columns(owner, c):
        return pl.ds(pl.multiple_of(owner * chans + c * LANES, LANES), LANES)

    def block_rows(owner):
        return pl.ds(pl.multiple_of(owner * share, share), share)

    def own_copy(a, c):
        source, target = ((tokens, tok_in), (cotangent, cot_in))[a]
        return pltpu.make_async_copy(
            source.at[:, columns(grp, c)], target.at[c, block_rows(grp), :], recv_sem.at[a, c, grp]
        )

    def block_copy(a, c, sender, receiver):
        source, target = ((tokens, tok_in), (cotangent, cot_in))[a]
        return pltpu.make_async_remote_copy(
            src_ref=source.at[:, columns(receiver, c)],
            dst_ref=target.at[c, block_rows(sender), :],
            send_sem=send_sem.at[a, c, receiver],
            recv_sem=recv_sem.at[a, c, sender],
            device_id=(ctx, receiver),
            device_id_type=MESH,
        )

    def send_chunk(c, _):
        for a in range(2):
            own_copy(a, c).start()
            for off in range(1, grps):
                block_copy(a, c, grp, lax.rem(grp + off, grps)).start()
        return 0

    lax.fori_loop(0, chunks, send_chunk, 0)

    @pl.when(first)
    def _():
        before[...] = jnp.zeros_like(before)

    @pl.when(last)
    def _():
        after[...] = jnp.zeros_like(after)
        cot_after[...] = jnp.zeros_like(cot_after)

    @pl.when(ctx > 0)
    def _():
        edge_copy(0, 0).wait_recv()

    @pl.when(ctx < ctxs - 1)
    def _():
        edge_copy(1, 0).wait_recv()
        edge_copy(2, 0).wait_recv()

    def state_copy(c, sender, receiver):
        return pltpu.make_async_remote_copy(
            src_ref=every.at[c, sender],
            dst_ref=every.at[c, sender],
            send_sem=state_send.at[c, receiver],
            recv_sem=state_recv.at[c, sender],
            device_id=(receiver, grp),
            device_id_type=MESH,
        )

    def here(c):
        return pl.ds(pl.multiple_of(c * LANES, LANES), LANES)

    def phase_one(c):
        slot = lax.rem(c, 2)
        for a in range(2):
            own_copy(a, c).wait()
            for off in range(1, grps):
                sender = lax.rem(grp + off, grps)
                block_copy(a, c, sender, sender).wait_recv()
        at = here(c)
        stage(rows, taps, before[:, at], tok_in[c], after[:, at], cot_in[c], cot_after[:, at],
              natural, cnat, xt, ct.at[slot])
        weights[...] = w_ref[:, :, at]
        convolve(length, taps, weights, xt, ct.at[slot], None, k_at.at[slot], v_at.at[slot],
                 src.at[slot], ups.at[slot])
        inverse = inv_ref[:, at]
        decay[...] = jnp.exp(-inverse)
        local_states(length, poles, decay, src.at[slot], ups.at[slot], ends, heads)
        total, head = link_segments(
            length, poles, inverse, ends, heads, starts.at[slot], nexts.at[slot]
        )
        every[c, ctx, 0] = total
        every[c, ctx, 1] = head
        for off in range(1, ctxs):
            state_copy(c, ctx, lax.rem(ctx + off, ctxs)).start()

    def phase_two(c):
        slot = lax.rem(c, 2)
        for off in range(1, ctxs):
            sender = lax.rem(ctx + off, ctxs)
            state_copy(c, sender, sender).wait_recv()
        at = here(c)
        weights[...] = w_ref[:, :, at]
        inverse = inv_ref[:, at]
        decay[...] = jnp.exp(-inverse)
        gain[...] = gain_ref[:, at]
        skip = skip_ref[:, at]
        over = jnp.exp(-float(rows) * inverse)
        incoming = jnp.zeros_like(inverse)
        later = jnp.zeros_like(inverse)
        for j in range(ctxs):
            incoming = jnp.where(j < ctx, over * incoming + every[c, j, 0], incoming)
            r = ctxs - 1 - j
            later = jnp.where(r > ctx, over * later + every[c, r, 1], later)
        enter(length, poles, inverse, incoming, later, starts.at[slot], nexts.at[slot], begin, finish)
        k_here, v_here, c_here = k_at.at[slot], v_at.at[slot], ct.at[slot]

        def store_q(t, value):
            dq[t] = c_here[t] * value

        def store_kv(t, value):
            k, v = k_here[t], v_here[t]
            k_here[t] = value * v
            v_here[t] = value * k

        mix(length, poles, False, decay, gain, skip, begin, src.at[slot], store_q)
        mix(length, poles, True, decay, gain, skip, finish, ups.at[slot], store_kv)
        gather_taps(length, taps, weights, (dq, k_here, v_here), natural)
        out[:, at] = natural[0:rows, :].astype(jnp.bfloat16)

    phase_one(0)

    def stagger(c, _):
        phase_one(c)
        phase_two(c - 1)
        return 0

    lax.fori_loop(1, chunks, stagger, 0)
    phase_two(chunks - 1)

    def drain(c, _):
        for a in range(2):
            for off in range(1, grps):
                block_copy(a, c, grp, lax.rem(grp + off, grps)).wait_send()
        for off in range(1, ctxs):
            state_copy(c, ctx, lax.rem(ctx + off, ctxs)).wait_send()
        return 0

    lax.fori_loop(0, chunks, drain, 0)

    @pl.when(sends_tail)
    def _():
        for j in range(grps):
            edge_copy(0, j).wait_send()

    @pl.when(sends_lead)
    def _():
        for j in range(grps):
            edge_copy(1, j).wait_send()
            edge_copy(2, j).wait_send()


def per_device(tokens, cotangent, conv_weight, residue, decay_length, skip_gain):
    ctxs, grps = lax.axis_size("ctx"), lax.axis_size("grp")
    poles, chans = residue.shape
    taps = conv_weight.shape[1]
    rows = tokens.shape[0] * grps
    length = rows // SEGS + 1
    chunks = chans // LANES
    inverse = 1.0 / decay_length
    gain = residue * jnp.sqrt(-jnp.expm1(-2.0 * inverse))
    f32, bf16 = jnp.float32, jnp.bfloat16

    def turned(*lead, extra=0):
        return pltpu.VMEM((*lead, length + extra, SEGS, LANES), f32)

    more = taps - 1
    vmem = pl.BlockSpec(memory_space=pltpu.VMEM)
    far = pl.BlockSpec(memory_space=pl.ANY)
    small = pltpu.VMEM((poles * SEGS, LANES), f32)
    pair = pltpu.VMEM((2, poles * SEGS, LANES), f32)
    linked = pltpu.VMEM((2, SEGS, poles, LANES), f32)
    edge = pltpu.VMEM((HALO, chans), bf16)
    arrived = pltpu.VMEM((chunks, rows, LANES), bf16)
    natural = pltpu.VMEM((rows + 2 * HALO, LANES), f32)
    dma = pltpu.SemaphoreType.DMA
    return pl.pallas_call(
        functools.partial(kernel, ctxs, grps, poles, taps),
        out_shape=jax.ShapeDtypeStruct((rows, chans), bf16),
        in_specs=[far, far, vmem, vmem, vmem, vmem],
        out_specs=vmem,
        scratch_shapes=[
            arrived, arrived, edge, edge, edge, pltpu.VMEM((chunks, ctxs, 2, poles, LANES), f32),
            natural, natural, turned(extra=more), turned(2),
            turned(2, extra=more), turned(2, extra=more), turned(2), turned(2), turned(extra=more),
            pltpu.VMEM((poles, LANES), f32), pltpu.VMEM((3, taps, LANES), f32),
            pltpu.VMEM((poles, LANES), f32), pair, pair, linked, linked, small, small,
            dma((2, chunks, grps)), dma((2, chunks, grps)), dma((3, grps)), dma((3,)),
            dma((chunks, ctxs)), dma((chunks, ctxs)),
        ],
        compiler_params=pltpu.CompilerParams(
            vmem_limit_bytes=56 * 2**20, collective_id=0, has_side_effects=True
        ),
    )(tokens, cotangent, conv_weight, inverse, gain, skip_gain[None])


def solution(mesh):
    placed = (
        P(("ctx", "grp"), None),
        P(("ctx", "grp"), None),
        P(None, None, "grp"),
        P(None, "grp"),
        P(None, "grp"),
        P("grp"),
    )
    return jax.shard_map(
        per_device, mesh=mesh, in_specs=placed, out_specs=P("ctx", "grp"), check_vma=False
    )
```

```python
import functools

import jax
import jax.numpy as jnp
from jax import lax
from jax.experimental import pallas as pl
from jax.experimental.pallas import tpu as pltpu
from jax.sharding import PartitionSpec as P

MESH = pl.DeviceIdType.MESH
LANES = 128
SEGS = 8
HALO = 16


def repeat(count, unroll, body, carry):
    whole = count // unroll

    def group(index, carried):
        for step in range(unroll):
            carried = body(index * unroll + step, carried)
        return carried

    carry = lax.fori_loop(0, whole, group, carry)
    for step in range(whole * unroll, count):
        carry = body(step, carry)
    return carry


def tree_sum(terms):
    terms = list(terms)
    while len(terms) > 1:
        terms = [
            terms[i] + terms[i + 1] if i + 1 < len(terms) else terms[i]
            for i in range(0, len(terms), 2)
        ]
    return terms[0]


def spread(row):
    return jnp.broadcast_to(row, (SEGS, LANES))


def relayout(natural, turned, first, count, length):
    def body(j, _):
        turned[j] = natural[pl.ds(first + j, SEGS, stride=length), :]
        return 0

    repeat(count, 8, body, 0)


def convolve(length, taps, w_ref, xt, ct, q_at, k_at, v_at, src, ups):
    weights = [[spread(w_ref[k, i : i + 1, :]) for i in range(taps)] for k in range(3)]

    def body(t, _):
        window = [xt[t + taps - 1 - i] for i in range(taps)]
        q, k, v = (tree_sum(weights[s][i] * window[i] for i in range(taps)) for s in range(3))
        if q_at is not None:
            q_at[t] = q
        if k_at is not None:
            k_at[t] = k
            v_at[t] = v
        src[t] = k * v
        ups[t] = q * ct[t]
        return 0

    repeat(length, 3, body, 0)


def local_states(length, poles, decay, src, ups, ends, heads):
    d = [spread(decay[p : p + 1, :]) for p in range(poles)]
    zero = jnp.zeros((SEGS, LANES), jnp.float32)

    def body(t, states):
        x, u = src[t], ups[length - 1 - t]
        return (
            tuple(d[p] * states[0][p] + x for p in range(poles)),
            tuple(d[p] * states[1][p] + u for p in range(poles)),
        )

    states = ((zero,) * poles, (zero,) * poles)
    short = length - SEGS
    states = repeat(short, 4, body, states)
    for p in range(poles):
        ends[1, p * SEGS : (p + 1) * SEGS, :] = states[0][p]
        heads[1, p * SEGS : (p + 1) * SEGS, :] = states[1][p]
    for t in range(SEGS):
        states = body(short + t, states)
    for p in range(poles):
        ends[0, p * SEGS : (p + 1) * SEGS, :] = states[0][p]
        heads[0, p * SEGS : (p + 1) * SEGS, :] = states[1][p]


def link_segments(length, poles, inverse, ends, heads, starts, nexts):
    over = jnp.exp(-float(length) * inverse)
    partial = jnp.exp(-float(length - SEGS) * inverse)
    carried = jnp.zeros_like(inverse)
    for s in range(SEGS):
        starts[s] = carried
        if s < SEGS - 1:
            carried = over * carried + ends[0, pl.ds(s, poles, stride=SEGS), :]
    total = partial * carried + ends[1, pl.ds(SEGS - 1, poles, stride=SEGS), :]
    carried = jnp.zeros_like(inverse)
    for s in reversed(range(SEGS)):
        nexts[s] = carried
        if s:
            carried = over * carried + heads[0, pl.ds(s, poles, stride=SEGS), :]
    return total, partial * carried + heads[1, pl.ds(0, poles, stride=SEGS), :]


def enter(length, poles, inverse, incoming, after, starts, nexts, begin, finish):
    for s in range(SEGS):
        begin[pl.ds(s, poles, stride=SEGS), :] = (
            starts[s] + jnp.exp(-float(s * length) * inverse) * incoming
        )
        finish[pl.ds(s, poles, stride=SEGS), :] = (
            nexts[s] + jnp.exp(-float((SEGS - 1 - s) * length) * inverse) * after
        )


def mix(length, poles, backward, decay, gain, skip, entering, stream, store):
    d = [spread(decay[p : p + 1, :]) for p in range(poles)]
    g = [spread(gain[p : p + 1, :]) for p in range(poles)]
    skip = spread(skip)
    states = tuple(entering[p * SEGS : (p + 1) * SEGS, :] for p in range(poles))

    def body(step, states):
        t = length - 1 - step if backward else step
        x = stream[t]
        states = tuple(d[p] * states[p] + x for p in range(poles))
        store(t, tree_sum([g[p] * states[p] for p in range(poles)] + [skip * x]))
        return states

    repeat(length, 4, body, states)


def gather_taps(length, taps, w_ref, streams, natural):
    weights = [[spread(w_ref[k, i : i + 1, :]) for i in range(taps)] for k in range(3)]
    for stream in streams:
        for j in range(taps - 1):
            stream[length + j] = pltpu.roll(stream[j], SEGS - 1, 0)

    def body(t, _):
        grad = tree_sum(
            tree_sum(weights[k][i] * streams[k][t + i] for i in range(taps)) for k in range(3)
        )
        natural[pl.ds(t, SEGS, stride=length), :] = grad
        return 0

    repeat(length, 3, body, 0)


def stage(rows, taps, before, tok, after, cot, cot_after, natural, cnat, xt, ct):
    length = rows // SEGS + 1
    natural[0:HALO, :] = before.astype(jnp.float32)
    natural[HALO : HALO + rows, :] = tok.astype(jnp.float32)
    natural[HALO + rows : HALO + rows + HALO, :] = after.astype(jnp.float32)
    cnat[0:rows, :] = cot.astype(jnp.float32)
    cnat[rows : rows + HALO, :] = cot_after.astype(jnp.float32)
    relayout(natural, xt, HALO - (taps - 1), length + taps - 1, length)
    relayout(cnat, ct, 0, length, length)


def kernel(ctxs, grps, poles, taps, tokens, cotangent, w_ref, inv_ref, gain_ref, skip_ref, out,
           tok_in, cot_in, before, after, cot_after, every,
           natural, cnat, xt, ct, k_at, v_at, src, ups, dq,
           decay, weights, gain, ends, heads, starts, nexts, begin, finish,
           send_sem, recv_sem, edge_send, edge_recv, state_send, state_recv):
    ctx, grp = lax.axis_index("ctx"), lax.axis_index("grp")
    share, chans = tokens.shape[0], out.shape[1]
    rows = share * grps
    length = rows // SEGS + 1
    chunks = chans // LANES
    first, last = ctx == 0, ctx == ctxs - 1
    lead, tail = grp == 0, grp == grps - 1

    barrier = pltpu.get_barrier_semaphore()

    def greet(to_ctx, to_grp):
        pl.semaphore_signal(barrier, inc=1, device_id=(to_ctx, to_grp), device_id_type=MESH)

    for off in range(1, grps):
        greet(ctx, lax.rem(grp + off, grps))
    for off in range(1, ctxs):
        greet(lax.rem(ctx + off, ctxs), grp)

    @pl.when(ctx > 0)
    def _():
        greet(ctx - 1, grps - 1)

    @pl.when(ctx < ctxs - 1)
    def _():
        greet(ctx + 1, 0)

    sends_tail = jnp.logical_and(tail, ctx < ctxs - 1)
    sends_lead = jnp.logical_and(lead, ctx > 0)
    edges = jnp.where(sends_tail, grps, 0) + jnp.where(sends_lead, grps, 0)
    pl.semaphore_wait(barrier, grps - 1 + ctxs - 1 + edges)

    def edge_copy(kind, j):
        source = (tokens, tokens, cotangent)[kind]
        row = share - HALO if kind == 0 else 0
        return pltpu.make_async_remote_copy(
            src_ref=source.at[row : row + HALO, pl.ds(pl.multiple_of(j * chans, LANES), chans)],
            dst_ref=(before, after, cot_after)[kind],
            send_sem=edge_send.at[kind, j],
            recv_sem=edge_recv.at[kind],
            device_id=(ctx + 1 if kind == 0 else ctx - 1, j),
            device_id_type=MESH,
        )

    @pl.when(sends_tail)
    def _():
        for j in range(grps):
            edge_copy(0, j).start()

    @pl.when(sends_lead)
    def _():
        for j in range(grps):
            edge_copy(1, j).start()
            edge_copy(2, j).start()

    def columns(owner, c):
        return pl.ds(pl.multiple_of(owner * chans + c * LANES, LANES), LANES)

    def block_rows(owner):
        return pl.ds(pl.multiple_of(owner * share, share), share)

    def own_copy(a, c):
        source, target = ((tokens, tok_in), (cotangent, cot_in))[a]
        return pltpu.make_async_copy(
            source.at[:, columns(grp, c)], target.at[c, block_rows(grp), :], recv_sem.at[a, c, grp]
        )

    def block_copy(a, c, sender, receiver):
        source, target = ((tokens, tok_in), (cotangent, cot_in))[a]
        return pltpu.make_async_remote_copy(
            src_ref=source.at[:, columns(receiver, c)],
            dst_ref=target.at[c, block_rows(sender), :],
            send_sem=send_sem.at[a, c, receiver],
            recv_sem=recv_sem.at[a, c, sender],
            device_id=(ctx, receiver),
            device_id_type=MESH,
        )

    def send_chunk(c, _):
        for a in range(2):
            own_copy(a, c).start()
            for off in range(1, grps):
                block_copy(a, c, grp, lax.rem(grp + off, grps)).start()
        return 0

    lax.fori_loop(0, min(2, chunks), send_chunk, 0)

    @pl.when(first)
    def _():
        before[...] = jnp.zeros_like(before)

    @pl.when(last)
    def _():
        after[...] = jnp.zeros_like(after)
        cot_after[...] = jnp.zeros_like(cot_after)

    @pl.when(ctx > 0)
    def _():
        edge_copy(0, 0).wait_recv()

    @pl.when(ctx < ctxs - 1)
    def _():
        edge_copy(1, 0).wait_recv()
        edge_copy(2, 0).wait_recv()

    def state_copy(c, sender, receiver):
        return pltpu.make_async_remote_copy(
            src_ref=every.at[c, sender],
            dst_ref=every.at[c, sender],
            send_sem=state_send.at[c, receiver],
            recv_sem=state_recv.at[c, sender],
            device_id=(receiver, grp),
            device_id_type=MESH,
        )

    def here(c):
        return pl.ds(pl.multiple_of(c * LANES, LANES), LANES)

    def phase_one(c):
        slot = lax.rem(c, 2)
        for a in range(2):
            own_copy(a, c).wait()
            for off in range(1, grps):
                sender = lax.rem(grp + off, grps)
                block_copy(a, c, sender, sender).wait_recv()
        at = here(c)
        stage(rows, taps, before[:, at], tok_in[c], after[:, at], cot_in[c], cot_after[:, at],
              natural, cnat, xt, ct.at[slot])
        weights[...] = w_ref[:, :, at]
        convolve(length, taps, weights, xt, ct.at[slot], None, k_at.at[slot], v_at.at[slot],
                 src.at[slot], ups.at[slot])
        inverse = inv_ref[:, at]
        decay[...] = jnp.exp(-inverse)
        local_states(length, poles, decay, src.at[slot], ups.at[slot], ends, heads)
        total, head = link_segments(
            length, poles, inverse, ends, heads, starts.at[slot], nexts.at[slot]
        )
        every[c, ctx, 0] = total
        every[c, ctx, 1] = head
        for off in range(1, ctxs):
            state_copy(c, ctx, lax.rem(ctx + off, ctxs)).start()

        @pl.when(c + 2 < chunks)
        def _():
            send_chunk(c + 2, 0)

    def phase_two(c):
        slot = lax.rem(c, 2)
        for off in range(1, ctxs):
            sender = lax.rem(ctx + off, ctxs)
            state_copy(c, sender, sender).wait_recv()
        at = here(c)
        weights[...] = w_ref[:, :, at]
        inverse = inv_ref[:, at]
        decay[...] = jnp.exp(-inverse)
        gain[...] = gain_ref[:, at]
        skip = skip_ref[:, at]
        over = jnp.exp(-float(rows) * inverse)
        incoming = jnp.zeros_like(inverse)
        later = jnp.zeros_like(inverse)
        for j in range(ctxs):
            incoming = jnp.where(j < ctx, over * incoming + every[c, j, 0], incoming)
            r = ctxs - 1 - j
            later = jnp.where(r > ctx, over * later + every[c, r, 1], later)
        enter(length, poles, inverse, incoming, later, starts.at[slot], nexts.at[slot], begin, finish)
        k_here, v_here, c_here = k_at.at[slot], v_at.at[slot], ct.at[slot]

        def store_q(t, value):
            dq[t] = c_here[t] * value

        def store_kv(t, value):
            k, v = k_here[t], v_here[t]
            k_here[t] = value * v
            v_here[t] = value * k

        mix(length, poles, False, decay, gain, skip, begin, src.at[slot], store_q)
        mix(length, poles, True, decay, gain, skip, finish, ups.at[slot], store_kv)
        gather_taps(length, taps, weights, (dq, k_here, v_here), natural)
        out[:, at] = natural[0:rows, :].astype(jnp.bfloat16)

    phase_one(jnp.int32(0))

    def stagger(c, _):
        phase_one(c)
        phase_two(c - 1)
        return 0

    lax.fori_loop(1, chunks, stagger, 0)
    phase_two(jnp.int32(chunks - 1))

    def drain(c, _):
        for a in range(2):
            for off in range(1, grps):
                block_copy(a, c, grp, lax.rem(grp + off, grps)).wait_send()
        for off in range(1, ctxs):
            state_copy(c, ctx, lax.rem(ctx + off, ctxs)).wait_send()
        return 0

    lax.fori_loop(0, chunks, drain, 0)

    @pl.when(sends_tail)
    def _():
        for j in range(grps):
            edge_copy(0, j).wait_send()

    @pl.when(sends_lead)
    def _():
        for j in range(grps):
            edge_copy(1, j).wait_send()
            edge_copy(2, j).wait_send()


def per_device(tokens, cotangent, conv_weight, residue, decay_length, skip_gain):
    ctxs, grps = lax.axis_size("ctx"), lax.axis_size("grp")
    poles, chans = residue.shape
    taps = conv_weight.shape[1]
    rows = tokens.shape[0] * grps
    length = rows // SEGS + 1
    chunks = chans // LANES
    inverse = 1.0 / decay_length
    gain = residue * jnp.sqrt(-jnp.expm1(-2.0 * inverse))
    f32, bf16 = jnp.float32, jnp.bfloat16

    def turned(*lead, extra=0):
        return pltpu.VMEM((*lead, length + extra, SEGS, LANES), f32)

    more = taps - 1
    vmem = pl.BlockSpec(memory_space=pltpu.VMEM)
    far = pl.BlockSpec(memory_space=pl.ANY)
    small = pltpu.VMEM((poles * SEGS, LANES), f32)
    pair = pltpu.VMEM((2, poles * SEGS, LANES), f32)
    linked = pltpu.VMEM((2, SEGS, poles, LANES), f32)
    edge = pltpu.VMEM((HALO, chans), bf16)
    arrived = pltpu.VMEM((chunks, rows, LANES), bf16)
    natural = pltpu.VMEM((rows + 2 * HALO, LANES), f32)
    dma = pltpu.SemaphoreType.DMA
    return pl.pallas_call(
        functools.partial(kernel, ctxs, grps, poles, taps),
        out_shape=jax.ShapeDtypeStruct((rows, chans), bf16),
        in_specs=[far, far, vmem, vmem, vmem, vmem],
        out_specs=vmem,
        scratch_shapes=[
            arrived, arrived, edge, edge, edge, pltpu.VMEM((chunks, ctxs, 2, poles, LANES), f32),
            natural, natural, turned(extra=more), turned(2),
            turned(2, extra=more), turned(2, extra=more), turned(2), turned(2), turned(extra=more),
            pltpu.VMEM((poles, LANES), f32), pltpu.VMEM((3, taps, LANES), f32),
            pltpu.VMEM((poles, LANES), f32), pair, pair, linked, linked, small, small,
            dma((2, chunks, grps)), dma((2, chunks, grps)), dma((3, grps)), dma((3,)),
            dma((chunks, ctxs)), dma((chunks, ctxs)),
        ],
        compiler_params=pltpu.CompilerParams(
            vmem_limit_bytes=56 * 2**20, collective_id=0, has_side_effects=True
        ),
    )(tokens, cotangent, conv_weight, inverse, gain, skip_gain[None])


def solution(mesh):
    placed = (
        P(("ctx", "grp"), None),
        P(("ctx", "grp"), None),
        P(None, None, "grp"),
        P(None, "grp"),
        P(None, "grp"),
        P("grp"),
    )
    return jax.shard_map(
        per_device, mesh=mesh, in_specs=placed, out_specs=P("ctx", "grp"), check_vma=False
    )
```

```python
import functools

import jax
import jax.numpy as jnp
from jax import lax
from jax.experimental import pallas as pl
from jax.experimental.pallas import tpu as pltpu
from jax.sharding import PartitionSpec as P

MESH = pl.DeviceIdType.MESH
LANES = 128
SEGS = 8
HALO = 16


def repeat(count, unroll, body, carry):
    whole = count // unroll

    def group(index, carried):
        for step in range(unroll):
            carried = body(index * unroll + step, carried)
        return carried

    carry = lax.fori_loop(0, whole, group, carry)
    for step in range(whole * unroll, count):
        carry = body(step, carry)
    return carry


def tree_sum(terms):
    terms = list(terms)
    while len(terms) > 1:
        terms = [
            terms[i] + terms[i + 1] if i + 1 < len(terms) else terms[i]
            for i in range(0, len(terms), 2)
        ]
    return terms[0]


def spread(row):
    return jnp.broadcast_to(row, (SEGS, LANES))


def relayout(natural, turned, first, count, length):
    def body(j, _):
        turned[j] = natural[pl.ds(first + j, SEGS, stride=length), :]
        return 0

    repeat(count, 8, body, 0)


def convolve(length, taps, w_ref, xt, q_at, k_at, v_at, src):
    weights = [[spread(w_ref[k, i : i + 1, :]) for i in range(taps)] for k in range(3)]

    def body(t, _):
        window = [xt[t + taps - 1 - i] for i in range(taps)]
        q, k, v = (tree_sum(weights[s][i] * window[i] for i in range(taps)) for s in range(3))
        q_at[t] = q
        k_at[t] = k
        v_at[t] = v
        src[t] = k * v
        return 0

    repeat(length, 3, body, 0)


def local_states(length, poles, decay, fetch, ends):
    d = [spread(decay[p : p + 1, :]) for p in range(poles)]
    zero = jnp.zeros((SEGS, LANES), jnp.float32)

    def body(step, states):
        x = fetch(step)
        return tuple(d[p] * states[p] + x for p in range(poles))

    short = length - SEGS
    states = repeat(short, 4, body, (zero,) * poles)
    for p in range(poles):
        ends[1, p * SEGS : (p + 1) * SEGS, :] = states[p]
    for t in range(SEGS):
        states = body(short + t, states)
    for p in range(poles):
        ends[0, p * SEGS : (p + 1) * SEGS, :] = states[p]


def link_segments(length, poles, order, inverse, ends, starts):
    over = jnp.exp(-float(length) * inverse)
    partial = jnp.exp(-float(length - SEGS) * inverse)
    carried = jnp.zeros_like(inverse)
    for s in order:
        starts[s] = carried
        if s != order[-1]:
            carried = over * carried + ends[0, pl.ds(s, poles, stride=SEGS), :]
    return partial * carried + ends[1, pl.ds(order[-1], poles, stride=SEGS), :]


def enter(length, poles, order, inverse, incoming, starts, begin):
    for rank, s in enumerate(order):
        begin[pl.ds(s, poles, stride=SEGS), :] = (
            starts[s] + jnp.exp(-float(rank * length) * inverse) * incoming
        )


def mix(length, poles, backward, decay, gain, skip, entering, stream, store):
    d = [spread(decay[p : p + 1, :]) for p in range(poles)]
    g = [spread(gain[p : p + 1, :]) for p in range(poles)]
    skip = spread(skip)
    states = tuple(entering[p * SEGS : (p + 1) * SEGS, :] for p in range(poles))

    def body(step, states):
        t = length - 1 - step if backward else step
        x = stream[t]
        states = tuple(d[p] * states[p] + x for p in range(poles))
        store(t, tree_sum([g[p] * states[p] for p in range(poles)] + [skip * x]))
        return states

    repeat(length, 4, body, states)


def gather_taps(length, taps, w_ref, streams, natural):
    weights = [[spread(w_ref[k, i : i + 1, :]) for i in range(taps)] for k in range(3)]
    for stream in streams:
        for j in range(taps - 1):
            stream[length + j] = pltpu.roll(stream[j], SEGS - 1, 0)

    def body(t, _):
        grad = tree_sum(
            tree_sum(weights[k][i] * streams[k][t + i] for i in range(taps)) for k in range(3)
        )
        natural[pl.ds(t, SEGS, stride=length), :] = grad
        return 0

    repeat(length, 3, body, 0)


def kernel(ctxs, grps, poles, taps, tokens, cotangent, w_ref, inv_ref, gain_ref, skip_ref, out,
           tok_in, cot_in, before, after, cot_after, every,
           natural, cnat, xt, q_at, k_at, v_at, src, ups, dq,
           decay, weights, gain, ends, starts, nexts, begin,
           send_sem, recv_sem, edge_send, edge_recv, state_send, state_recv):
    ctx, grp = lax.axis_index("ctx"), lax.axis_index("grp")
    share, chans = tokens.shape[0], out.shape[1]
    rows = share * grps
    length = rows // SEGS + 1
    chunks = chans // LANES
    first, last = ctx == 0, ctx == ctxs - 1
    lead, tail = grp == 0, grp == grps - 1

    barrier = pltpu.get_barrier_semaphore()

    def greet(to_ctx, to_grp):
        pl.semaphore_signal(barrier, inc=1, device_id=(to_ctx, to_grp), device_id_type=MESH)

    for off in range(1, grps):
        greet(ctx, lax.rem(grp + off, grps))
    for off in range(1, ctxs):
        greet(lax.rem(ctx + off, ctxs), grp)

    @pl.when(ctx > 0)
    def _():
        greet(ctx - 1, grps - 1)

    @pl.when(ctx < ctxs - 1)
    def _():
        greet(ctx + 1, 0)

    sends_tail = jnp.logical_and(tail, ctx < ctxs - 1)
    sends_lead = jnp.logical_and(lead, ctx > 0)
    edges = jnp.where(sends_tail, grps, 0) + jnp.where(sends_lead, grps, 0)
    pl.semaphore_wait(barrier, grps - 1 + ctxs - 1 + edges)

    def edge_copy(kind, j):
        source = (tokens, tokens, cotangent)[kind]
        row = share - HALO if kind == 0 else 0
        return pltpu.make_async_remote_copy(
            src_ref=source.at[row : row + HALO, pl.ds(pl.multiple_of(j * chans, LANES), chans)],
            dst_ref=(before, after, cot_after)[kind],
            send_sem=edge_send.at[kind, j],
            recv_sem=edge_recv.at[kind],
            device_id=(ctx + 1 if kind == 0 else ctx - 1, j),
            device_id_type=MESH,
        )

    @pl.when(sends_tail)
    def _():
        for j in range(grps):
            edge_copy(0, j).start()

    @pl.when(sends_lead)
    def _():
        for j in range(grps):
            edge_copy(1, j).start()
            edge_copy(2, j).start()

    def columns(owner, c):
        return pl.ds(pl.multiple_of(owner * chans + c * LANES, LANES), LANES)

    def block_rows(owner):
        return pl.ds(pl.multiple_of(owner * share, share), share)

    def own_copy(a, c):
        source, target = ((tokens, tok_in), (cotangent, cot_in))[a]
        return pltpu.make_async_copy(
            source.at[:, columns(grp, c)], target.at[c, block_rows(grp), :], recv_sem.at[a, c, grp]
        )

    def block_copy(a, c, sender, receiver):
        source, target = ((tokens, tok_in), (cotangent, cot_in))[a]
        return pltpu.make_async_remote_copy(
            src_ref=source.at[:, columns(receiver, c)],
            dst_ref=target.at[c, block_rows(sender), :],
            send_sem=send_sem.at[a, c, receiver],
            recv_sem=recv_sem.at[a, c, sender],
            device_id=(ctx, receiver),
            device_id_type=MESH,
        )

    def send_chunk(c, _):
        for a in range(2):
            own_copy(a, c).start()
            for off in range(1, grps):
                block_copy(a, c, grp, lax.rem(grp + off, grps)).start()
        return 0

    lax.fori_loop(0, chunks, send_chunk, 0)

    @pl.when(first)
    def _():
        before[...] = jnp.zeros_like(before)

    @pl.when(last)
    def _():
        after[...] = jnp.zeros_like(after)
        cot_after[...] = jnp.zeros_like(cot_after)

    @pl.when(ctx > 0)
    def _():
        edge_copy(0, 0).wait_recv()

    @pl.when(ctx < ctxs - 1)
    def _():
        edge_copy(1, 0).wait_recv()
        edge_copy(2, 0).wait_recv()

    def state_copy(kind, c, sender, receiver):
        return pltpu.make_async_remote_copy(
            src_ref=every.at[kind, c, sender],
            dst_ref=every.at[kind, c, sender],
            send_sem=state_send.at[kind, c, receiver],
            recv_sem=state_recv.at[kind, c, sender],
            device_id=(receiver, grp),
            device_id_type=MESH,
        )

    ahead, behind = tuple(range(SEGS)), tuple(reversed(range(SEGS)))

    def here(c):
        return pl.ds(pl.multiple_of(c * LANES, LANES), LANES)

    def arrive(a, c):
        own_copy(a, c).wait()
        for off in range(1, grps):
            sender = lax.rem(grp + off, grps)
            block_copy(a, c, sender, sender).wait_recv()

    def tell(kind, c, total):
        every[kind, c, ctx] = total
        for off in range(1, ctxs):
            state_copy(kind, c, ctx, lax.rem(ctx + off, ctxs)).start()

    def hear(kind, c, inverse):
        for off in range(1, ctxs):
            sender = lax.rem(ctx + off, ctxs)
            state_copy(kind, c, sender, sender).wait_recv()
        over = jnp.exp(-float(rows) * inverse)
        incoming = jnp.zeros_like(inverse)
        for j in range(ctxs):
            if kind == 0:
                incoming = jnp.where(j < ctx, over * incoming + every[0, c, j], incoming)
            else:
                r = ctxs - 1 - j
                incoming = jnp.where(r > ctx, over * incoming + every[1, c, r], incoming)
        return incoming

    def token_phase(c):
        slot, at = lax.rem(c, 2), here(c)
        arrive(0, c)
        natural[0:HALO, :] = before[:, at].astype(jnp.float32)
        natural[HALO : HALO + rows, :] = tok_in[c].astype(jnp.float32)
        natural[HALO + rows : HALO + rows + HALO, :] = after[:, at].astype(jnp.float32)
        relayout(natural, xt, HALO - (taps - 1), length + taps - 1, length)
        weights[...] = w_ref[:, :, at]
        convolve(length, taps, weights, xt, q_at, k_at.at[slot], v_at.at[slot], src)
        inverse = inv_ref[:, at]
        decay[...] = jnp.exp(-inverse)
        local_states(length, poles, decay, lambda t: src[t], ends)
        tell(0, c, link_segments(length, poles, ahead, inverse, ends, starts))

    def forward_phase(c):
        at = here(c)
        inverse = inv_ref[:, at]
        decay[...] = jnp.exp(-inverse)
        gain[...] = gain_ref[:, at]
        enter(length, poles, ahead, inverse, hear(0, c, inverse), starts, begin)

        def store(t, value):
            dq[t] = value

        mix(length, poles, False, decay, gain, skip_ref[:, at], begin, src, store)

    def cotangent_phase(c):
        at = here(c)
        arrive(1, c)
        cnat[0:rows, :] = cot_in[c].astype(jnp.float32)
        cnat[rows : rows + HALO, :] = cot_after[:, at].astype(jnp.float32)
        inverse = inv_ref[:, at]
        decay[...] = jnp.exp(-inverse)

        def fetch(step):
            t = length - 1 - step
            value = cnat[pl.ds(t, SEGS, stride=length), :]
            upstream = value * q_at[t]
            ups[t] = upstream
            dq[t] = dq[t] * value
            return upstream

        local_states(length, poles, decay, fetch, ends)
        tell(1, c, link_segments(length, poles, behind, inverse, ends, nexts))

    def gradient_phase(c):
        slot, at = lax.rem(c, 2), here(c)
        weights[...] = w_ref[:, :, at]
        inverse = inv_ref[:, at]
        decay[...] = jnp.exp(-inverse)
        gain[...] = gain_ref[:, at]
        enter(length, poles, behind, inverse, hear(1, c, inverse), nexts, begin)
        k_here, v_here = k_at.at[slot], v_at.at[slot]

        def store(t, value):
            k, v = k_here[t], v_here[t]
            k_here[t] = value * v
            v_here[t] = value * k

        mix(length, poles, True, decay, gain, skip_ref[:, at], begin, ups, store)
        gather_taps(length, taps, weights, (dq, k_here, v_here), natural)
        out[:, at] = natural[0:rows, :].astype(jnp.bfloat16)

    def turn(c, _):
        token_phase(c)

        @pl.when(c > 0)
        def _():
            gradient_phase(c - 1)

        forward_phase(c)
        cotangent_phase(c)
        return 0

    lax.fori_loop(0, chunks, turn, 0)
    gradient_phase(jnp.int32(chunks - 1))

    def drain(c, _):
        for a in range(2):
            for off in range(1, grps):
                block_copy(a, c, grp, lax.rem(grp + off, grps)).wait_send()
            for off in range(1, ctxs):
                state_copy(a, c, ctx, lax.rem(ctx + off, ctxs)).wait_send()
        return 0

    lax.fori_loop(0, chunks, drain, 0)

    @pl.when(sends_tail)
    def _():
        for j in range(grps):
            edge_copy(0, j).wait_send()

    @pl.when(sends_lead)
    def _():
        for j in range(grps):
            edge_copy(1, j).wait_send()
            edge_copy(2, j).wait_send()


def per_device(tokens, cotangent, conv_weight, residue, decay_length, skip_gain):
    ctxs, grps = lax.axis_size("ctx"), lax.axis_size("grp")
    poles, chans = residue.shape
    taps = conv_weight.shape[1]
    rows = tokens.shape[0] * grps
    length = rows // SEGS + 1
    chunks = chans // LANES
    inverse = 1.0 / decay_length
    gain = residue * jnp.sqrt(-jnp.expm1(-2.0 * inverse))
    f32, bf16 = jnp.float32, jnp.bfloat16

    def turned(*lead, extra=0):
        return pltpu.VMEM((*lead, length + extra, SEGS, LANES), f32)

    more = taps - 1
    vmem = pl.BlockSpec(memory_space=pltpu.VMEM)
    far = pl.BlockSpec(memory_space=pl.ANY)
    small = pltpu.VMEM((poles * SEGS, LANES), f32)
    pair = pltpu.VMEM((2, poles * SEGS, LANES), f32)
    linked = pltpu.VMEM((SEGS, poles, LANES), f32)
    edge = pltpu.VMEM((HALO, chans), bf16)
    arrived = pltpu.VMEM((chunks, rows, LANES), bf16)
    natural = pltpu.VMEM((rows + 2 * HALO, LANES), f32)
    dma = pltpu.SemaphoreType.DMA
    return pl.pallas_call(
        functools.partial(kernel, ctxs, grps, poles, taps),
        out_shape=jax.ShapeDtypeStruct((rows, chans), bf16),
        in_specs=[far, far, vmem, vmem, vmem, vmem],
        out_specs=vmem,
        scratch_shapes=[
            arrived, arrived, edge, edge, edge, pltpu.VMEM((2, chunks, ctxs, poles, LANES), f32),
            natural, natural, turned(extra=more), turned(),
            turned(2, extra=more), turned(2, extra=more), turned(), turned(), turned(extra=more),
            pltpu.VMEM((poles, LANES), f32), pltpu.VMEM((3, taps, LANES), f32),
            pltpu.VMEM((poles, LANES), f32), pair, linked, linked, small,
            dma((2, chunks, grps)), dma((2, chunks, grps)), dma((3, grps)), dma((3,)),
            dma((2, chunks, ctxs)), dma((2, chunks, ctxs)),
        ],
        compiler_params=pltpu.CompilerParams(
            vmem_limit_bytes=56 * 2**20, collective_id=0, has_side_effects=True
        ),
    )(tokens, cotangent, conv_weight, inverse, gain, skip_gain[None])


def solution(mesh):
    placed = (
        P(("ctx", "grp"), None),
        P(("ctx", "grp"), None),
        P(None, None, "grp"),
        P(None, "grp"),
        P(None, "grp"),
        P("grp"),
    )
    return jax.shard_map(
        per_device, mesh=mesh, in_specs=placed, out_specs=P("ctx", "grp"), check_vma=False
    )
```

```python
import functools

import jax
import jax.numpy as jnp
from jax import lax
from jax.experimental import pallas as pl
from jax.experimental.pallas import tpu as pltpu
from jax.sharding import PartitionSpec as P

MESH = pl.DeviceIdType.MESH
LANES = 128
SEGS = 8
HALO = 16


def repeat(count, unroll, body, carry):
    whole = count // unroll

    def group(index, carried):
        for step in range(unroll):
            carried = body(index * unroll + step, carried)
        return carried

    carry = lax.fori_loop(0, whole, group, carry)
    for step in range(whole * unroll, count):
        carry = body(step, carry)
    return carry


def tree_sum(terms):
    terms = list(terms)
    while len(terms) > 1:
        terms = [
            terms[i] + terms[i + 1] if i + 1 < len(terms) else terms[i]
            for i in range(0, len(terms), 2)
        ]
    return terms[0]


def spread(row):
    return jnp.broadcast_to(row, (SEGS, LANES))


def relayout(natural, turned, first, count, length):
    def body(j, _):
        turned[j] = natural[pl.ds(first + j, SEGS, stride=length), :]
        return 0

    repeat(count, 8, body, 0)


def convolve(length, taps, w_ref, xt, q_at, k_at, v_at, src):
    weights = [[spread(w_ref[k, i : i + 1, :]) for i in range(taps)] for k in range(3)]

    def body(t, _):
        window = [xt[t + taps - 1 - i] for i in range(taps)]
        q, k, v = (tree_sum(weights[s][i] * window[i] for i in range(taps)) for s in range(3))
        q_at[t] = q
        k_at[t] = k
        v_at[t] = v
        src[t] = k * v
        return 0

    repeat(length, 3, body, 0)


def local_states(length, poles, decay, fetch, ends):
    d = [spread(decay[p : p + 1, :]) for p in range(poles)]
    zero = jnp.zeros((SEGS, LANES), jnp.float32)

    def body(step, states):
        x = fetch(step)
        return tuple(d[p] * states[p] + x for p in range(poles))

    short = length - SEGS
    states = repeat(short, 4, body, (zero,) * poles)
    for p in range(poles):
        ends[1, p * SEGS : (p + 1) * SEGS, :] = states[p]
    for t in range(SEGS):
        states = body(short + t, states)
    for p in range(poles):
        ends[0, p * SEGS : (p + 1) * SEGS, :] = states[p]


def link_segments(length, poles, order, inverse, ends, starts):
    over = jnp.exp(-float(length) * inverse)
    partial = jnp.exp(-float(length - SEGS) * inverse)
    carried = jnp.zeros_like(inverse)
    for s in order:
        starts[s] = carried
        if s != order[-1]:
            carried = over * carried + ends[0, pl.ds(s, poles, stride=SEGS), :]
    return partial * carried + ends[1, pl.ds(order[-1], poles, stride=SEGS), :]


def enter(length, poles, order, inverse, incoming, starts, begin):
    for rank, s in enumerate(order):
        begin[pl.ds(s, poles, stride=SEGS), :] = (
            starts[s] + jnp.exp(-float(rank * length) * inverse) * incoming
        )


def mix(length, poles, backward, decay, gain, skip, entering, stream, store):
    d = [spread(decay[p : p + 1, :]) for p in range(poles)]
    g = [spread(gain[p : p + 1, :]) for p in range(poles)]
    skip = spread(skip)
    states = tuple(entering[p * SEGS : (p + 1) * SEGS, :] for p in range(poles))

    def body(step, states):
        t = length - 1 - step if backward else step
        x = stream[t]
        states = tuple(d[p] * states[p] + x for p in range(poles))
        store(t, tree_sum([g[p] * states[p] for p in range(poles)] + [skip * x]))
        return states

    repeat(length, 4, body, states)


def gather_taps(length, taps, w_ref, streams, natural):
    weights = [[spread(w_ref[k, i : i + 1, :]) for i in range(taps)] for k in range(3)]
    for stream in streams:
        for j in range(taps - 1):
            stream[length + j] = pltpu.roll(stream[j], SEGS - 1, 0)

    def body(t, _):
        grad = tree_sum(
            tree_sum(weights[k][i] * streams[k][t + i] for i in range(taps)) for k in range(3)
        )
        natural[pl.ds(t, SEGS, stride=length), :] = grad
        return 0

    repeat(length, 3, body, 0)


def kernel(ctxs, grps, poles, taps, tokens, cotangent, w_ref, inv_ref, gain_ref, skip_ref, out,
           tok_in, cot_in, before, after, cot_after, every,
           natural, cnat, xt, q_at, k_at, v_at, src, ups, dq,
           decay, weights, gain, ends, starts, nexts, begin,
           send_sem, recv_sem, edge_send, edge_recv, state_send, state_recv):
    ctx, grp = lax.axis_index("ctx"), lax.axis_index("grp")
    share, chans = tokens.shape[0], out.shape[1]
    rows = share * grps
    length = rows // SEGS + 1
    chunks = chans // LANES
    first, last = ctx == 0, ctx == ctxs - 1
    lead, tail = grp == 0, grp == grps - 1

    barrier = pltpu.get_barrier_semaphore()

    def greet(to_ctx, to_grp):
        pl.semaphore_signal(barrier, inc=1, device_id=(to_ctx, to_grp), device_id_type=MESH)

    for off in range(1, grps):
        greet(ctx, lax.rem(grp + off, grps))
    for off in range(1, ctxs):
        greet(lax.rem(ctx + off, ctxs), grp)

    @pl.when(ctx > 0)
    def _():
        greet(ctx - 1, grps - 1)

    @pl.when(ctx < ctxs - 1)
    def _():
        greet(ctx + 1, 0)

    sends_tail = jnp.logical_and(tail, ctx < ctxs - 1)
    sends_lead = jnp.logical_and(lead, ctx > 0)
    edges = jnp.where(sends_tail, grps, 0) + jnp.where(sends_lead, grps, 0)
    pl.semaphore_wait(barrier, grps - 1 + ctxs - 1 + edges)

    def edge_copy(kind, j):
        source = (tokens, tokens, cotangent)[kind]
        row = share - HALO if kind == 0 else 0
        return pltpu.make_async_remote_copy(
            src_ref=source.at[row : row + HALO, pl.ds(pl.multiple_of(j * chans, LANES), chans)],
            dst_ref=(before, after, cot_after)[kind],
            send_sem=edge_send.at[kind, j],
            recv_sem=edge_recv.at[kind],
            device_id=(ctx + 1 if kind == 0 else ctx - 1, j),
            device_id_type=MESH,
        )

    @pl.when(sends_tail)
    def _():
        for j in range(grps):
            edge_copy(0, j).start()

    @pl.when(sends_lead)
    def _():
        for j in range(grps):
            edge_copy(1, j).start()
            edge_copy(2, j).start()

    def columns(owner, c):
        return pl.ds(pl.multiple_of(owner * chans + c * LANES, LANES), LANES)

    def block_rows(owner):
        return pl.ds(pl.multiple_of(owner * share, share), share)

    def own_copy(a, c):
        source, target = ((tokens, tok_in), (cotangent, cot_in))[a]
        return pltpu.make_async_copy(
            source.at[:, columns(grp, c)], target.at[c, block_rows(grp), :], recv_sem.at[a, c, grp]
        )

    def block_copy(a, c, sender, receiver):
        source, target = ((tokens, tok_in), (cotangent, cot_in))[a]
        return pltpu.make_async_remote_copy(
            src_ref=source.at[:, columns(receiver, c)],
            dst_ref=target.at[c, block_rows(sender), :],
            send_sem=send_sem.at[a, c, receiver],
            recv_sem=recv_sem.at[a, c, sender],
            device_id=(ctx, receiver),
            device_id_type=MESH,
        )

    def send_blocks(a, c):
        own_copy(a, c).start()
        for off in range(1, grps):
            block_copy(a, c, grp, lax.rem(grp + off, grps)).start()

    def send_next(a, c):
        @pl.when(c + 1 < chunks)
        def _():
            send_blocks(a, c + 1)

    send_blocks(0, 0)
    send_blocks(1, 0)

    @pl.when(first)
    def _():
        before[...] = jnp.zeros_like(before)

    @pl.when(last)
    def _():
        after[...] = jnp.zeros_like(after)
        cot_after[...] = jnp.zeros_like(cot_after)

    @pl.when(ctx > 0)
    def _():
        edge_copy(0, 0).wait_recv()

    @pl.when(ctx < ctxs - 1)
    def _():
        edge_copy(1, 0).wait_recv()
        edge_copy(2, 0).wait_recv()

    def state_copy(kind, c, sender, receiver):
        return pltpu.make_async_remote_copy(
            src_ref=every.at[kind, c, sender],
            dst_ref=every.at[kind, c, sender],
            send_sem=state_send.at[kind, c, receiver],
            recv_sem=state_recv.at[kind, c, sender],
            device_id=(receiver, grp),
            device_id_type=MESH,
        )

    ahead, behind = tuple(range(SEGS)), tuple(reversed(range(SEGS)))

    def here(c):
        return pl.ds(pl.multiple_of(c * LANES, LANES), LANES)

    def arrive(a, c):
        own_copy(a, c).wait()
        for off in range(1, grps):
            sender = lax.rem(grp + off, grps)
            block_copy(a, c, sender, sender).wait_recv()

    def tell(kind, c, total):
        every[kind, c, ctx] = total
        for off in range(1, ctxs):
            state_copy(kind, c, ctx, lax.rem(ctx + off, ctxs)).start()

    def hear(kind, c, inverse):
        for off in range(1, ctxs):
            sender = lax.rem(ctx + off, ctxs)
            state_copy(kind, c, sender, sender).wait_recv()
        over = jnp.exp(-float(rows) * inverse)
        incoming = jnp.zeros_like(inverse)
        for j in range(ctxs):
            if kind == 0:
                incoming = jnp.where(j < ctx, over * incoming + every[0, c, j], incoming)
            else:
                r = ctxs - 1 - j
                incoming = jnp.where(r > ctx, over * incoming + every[1, c, r], incoming)
        return incoming

    def token_phase(c):
        slot, at = lax.rem(c, 2), here(c)
        arrive(0, c)
        send_next(0, c)
        natural[0:HALO, :] = before[:, at].astype(jnp.float32)
        natural[HALO : HALO + rows, :] = tok_in[c].astype(jnp.float32)
        natural[HALO + rows : HALO + rows + HALO, :] = after[:, at].astype(jnp.float32)
        relayout(natural, xt, HALO - (taps - 1), length + taps - 1, length)
        weights[...] = w_ref[:, :, at]
        convolve(length, taps, weights, xt, q_at, k_at.at[slot], v_at.at[slot], src)
        inverse = inv_ref[:, at]
        decay[...] = jnp.exp(-inverse)
        local_states(length, poles, decay, lambda t: src[t], ends)
        tell(0, c, link_segments(length, poles, ahead, inverse, ends, starts))

    def forward_phase(c):
        at = here(c)
        inverse = inv_ref[:, at]
        decay[...] = jnp.exp(-inverse)
        gain[...] = gain_ref[:, at]
        enter(length, poles, ahead, inverse, hear(0, c, inverse), starts, begin)

        def store(t, value):
            dq[t] = value

        mix(length, poles, False, decay, gain, skip_ref[:, at], begin, src, store)

    def cotangent_phase(c):
        at = here(c)
        arrive(1, c)
        send_next(1, c)
        cnat[0:rows, :] = cot_in[c].astype(jnp.float32)
        cnat[rows : rows + HALO, :] = cot_after[:, at].astype(jnp.float32)
        inverse = inv_ref[:, at]
        decay[...] = jnp.exp(-inverse)

        def fetch(step):
            t = length - 1 - step
            value = cnat[pl.ds(t, SEGS, stride=length), :]
            upstream = value * q_at[t]
            ups[t] = upstream
            dq[t] = dq[t] * value
            return upstream

        local_states(length, poles, decay, fetch, ends)
        tell(1, c, link_segments(length, poles, behind, inverse, ends, nexts))

    def gradient_phase(c):
        slot, at = lax.rem(c, 2), here(c)
        weights[...] = w_ref[:, :, at]
        inverse = inv_ref[:, at]
        decay[...] = jnp.exp(-inverse)
        gain[...] = gain_ref[:, at]
        enter(length, poles, behind, inverse, hear(1, c, inverse), nexts, begin)
        k_here, v_here = k_at.at[slot], v_at.at[slot]

        def store(t, value):
            k, v = k_here[t], v_here[t]
            k_here[t] = value * v
            v_here[t] = value * k

        mix(length, poles, True, decay, gain, skip_ref[:, at], begin, ups, store)
        gather_taps(length, taps, weights, (dq, k_here, v_here), natural)
        out[:, at] = natural[0:rows, :].astype(jnp.bfloat16)

    def turn(c, _):
        token_phase(c)

        @pl.when(c > 0)
        def _():
            gradient_phase(c - 1)

        forward_phase(c)
        cotangent_phase(c)
        return 0

    lax.fori_loop(0, chunks, turn, 0)
    gradient_phase(jnp.int32(chunks - 1))

    def drain(c, _):
        for a in range(2):
            for off in range(1, grps):
                block_copy(a, c, grp, lax.rem(grp + off, grps)).wait_send()
            for off in range(1, ctxs):
                state_copy(a, c, ctx, lax.rem(ctx + off, ctxs)).wait_send()
        return 0

    lax.fori_loop(0, chunks, drain, 0)

    @pl.when(sends_tail)
    def _():
        for j in range(grps):
            edge_copy(0, j).wait_send()

    @pl.when(sends_lead)
    def _():
        for j in range(grps):
            edge_copy(1, j).wait_send()
            edge_copy(2, j).wait_send()


def per_device(tokens, cotangent, conv_weight, residue, decay_length, skip_gain):
    ctxs, grps = lax.axis_size("ctx"), lax.axis_size("grp")
    poles, chans = residue.shape
    taps = conv_weight.shape[1]
    rows = tokens.shape[0] * grps
    length = rows // SEGS + 1
    chunks = chans // LANES
    inverse = 1.0 / decay_length
    gain = residue * jnp.sqrt(-jnp.expm1(-2.0 * inverse))
    f32, bf16 = jnp.float32, jnp.bfloat16

    def turned(*lead, extra=0):
        return pltpu.VMEM((*lead, length + extra, SEGS, LANES), f32)

    more = taps - 1
    vmem = pl.BlockSpec(memory_space=pltpu.VMEM)
    far = pl.BlockSpec(memory_space=pl.ANY)
    small = pltpu.VMEM((poles * SEGS, LANES), f32)
    pair = pltpu.VMEM((2, poles * SEGS, LANES), f32)
    linked = pltpu.VMEM((SEGS, poles, LANES), f32)
    edge = pltpu.VMEM((HALO, chans), bf16)
    arrived = pltpu.VMEM((chunks, rows, LANES), bf16)
    natural = pltpu.VMEM((rows + 2 * HALO, LANES), f32)
    dma = pltpu.SemaphoreType.DMA
    return pl.pallas_call(
        functools.partial(kernel, ctxs, grps, poles, taps),
        out_shape=jax.ShapeDtypeStruct((rows, chans), bf16),
        in_specs=[far, far, vmem, vmem, vmem, vmem],
        out_specs=vmem,
        scratch_shapes=[
            arrived, arrived, edge, edge, edge, pltpu.VMEM((2, chunks, ctxs, poles, LANES), f32),
            natural, natural, turned(extra=more), turned(),
            turned(2, extra=more), turned(2, extra=more), turned(), turned(), turned(extra=more),
            pltpu.VMEM((poles, LANES), f32), pltpu.VMEM((3, taps, LANES), f32),
            pltpu.VMEM((poles, LANES), f32), pair, linked, linked, small,
            dma((2, chunks, grps)), dma((2, chunks, grps)), dma((3, grps)), dma((3,)),
            dma((2, chunks, ctxs)), dma((2, chunks, ctxs)),
        ],
        compiler_params=pltpu.CompilerParams(
            vmem_limit_bytes=56 * 2**20, collective_id=0, has_side_effects=True
        ),
    )(tokens, cotangent, conv_weight, inverse, gain, skip_gain[None])


def solution(mesh):
    placed = (
        P(("ctx", "grp"), None),
        P(("ctx", "grp"), None),
        P(None, None, "grp"),
        P(None, "grp"),
        P(None, "grp"),
        P("grp"),
    )
    return jax.shard_map(
        per_device, mesh=mesh, in_specs=placed, out_specs=P("ctx", "grp"), check_vma=False
    )
```

```python
import functools

import jax
import jax.numpy as jnp
from jax import lax
from jax.experimental import pallas as pl
from jax.experimental.pallas import tpu as pltpu
from jax.sharding import PartitionSpec as P

MESH = pl.DeviceIdType.MESH
LANES = 128
SEGS = 8
HALO = 16


def repeat(count, unroll, body, carry):
    whole = count // unroll

    def group(index, carried):
        for step in range(unroll):
            carried = body(index * unroll + step, carried)
        return carried

    carry = lax.fori_loop(0, whole, group, carry)
    for step in range(whole * unroll, count):
        carry = body(step, carry)
    return carry


def tree_sum(terms):
    terms = list(terms)
    while len(terms) > 1:
        terms = [
            terms[i] + terms[i + 1] if i + 1 < len(terms) else terms[i]
            for i in range(0, len(terms), 2)
        ]
    return terms[0]


def spread(row):
    return jnp.broadcast_to(row, (SEGS, LANES))


def relayout(natural, turned, first, count, length):
    def body(j, _):
        turned[j] = natural[pl.ds(first + j, SEGS, stride=length), :]
        return 0

    repeat(count, 8, body, 0)


def convolve(length, taps, w_ref, xt, q_at, k_at, v_at, src):
    weights = [[spread(w_ref[k, i : i + 1, :]) for i in range(taps)] for k in range(3)]

    def body(t, _):
        window = [xt[t + taps - 1 - i] for i in range(taps)]
        q, k, v = (tree_sum(weights[s][i] * window[i] for i in range(taps)) for s in range(3))
        q_at[t] = q
        k_at[t] = k
        v_at[t] = v
        src[t] = k * v
        return 0

    repeat(length, 3, body, 0)


def local_states(length, poles, decay, fetch, ends):
    d = [spread(decay[p : p + 1, :]) for p in range(poles)]
    zero = jnp.zeros((SEGS, LANES), jnp.float32)

    def body(step, states):
        x = fetch(step)
        return tuple(d[p] * states[p] + x for p in range(poles))

    short = length - SEGS
    states = repeat(short, 8, body, (zero,) * poles)
    for p in range(poles):
        ends[1, p * SEGS : (p + 1) * SEGS, :] = states[p]
    for t in range(SEGS):
        states = body(short + t, states)
    for p in range(poles):
        ends[0, p * SEGS : (p + 1) * SEGS, :] = states[p]


def link_segments(length, poles, order, inverse, ends, starts):
    over = jnp.exp(-float(length) * inverse)
    partial = jnp.exp(-float(length - SEGS) * inverse)
    carried = jnp.zeros_like(inverse)
    for s in order:
        starts[s] = carried
        if s != order[-1]:
            carried = over * carried + ends[0, pl.ds(s, poles, stride=SEGS), :]
    return partial * carried + ends[1, pl.ds(order[-1], poles, stride=SEGS), :]


def enter(length, poles, order, inverse, incoming, starts, begin):
    for rank, s in enumerate(order):
        begin[pl.ds(s, poles, stride=SEGS), :] = (
            starts[s] + jnp.exp(-float(rank * length) * inverse) * incoming
        )


def mix(length, poles, backward, decay, gain, skip, entering, stream, store):
    d = [spread(decay[p : p + 1, :]) for p in range(poles)]
    g = [spread(gain[p : p + 1, :]) for p in range(poles)]
    skip = spread(skip)
    states = tuple(entering[p * SEGS : (p + 1) * SEGS, :] for p in range(poles))

    def body(step, states):
        t = length - 1 - step if backward else step
        x = stream[t]
        states = tuple(d[p] * states[p] + x for p in range(poles))
        store(t, tree_sum([g[p] * states[p] for p in range(poles)] + [skip * x]))
        return states

    repeat(length, 8, body, states)


def gather_taps(length, taps, w_ref, streams, natural):
    weights = [[spread(w_ref[k, i : i + 1, :]) for i in range(taps)] for k in range(3)]
    for stream in streams:
        for j in range(taps - 1):
            stream[length + j] = pltpu.roll(stream[j], SEGS - 1, 0)

    def body(t, _):
        grad = tree_sum(
            tree_sum(weights[k][i] * streams[k][t + i] for i in range(taps)) for k in range(3)
        )
        natural[pl.ds(t, SEGS, stride=length), :] = grad
        return 0

    repeat(length, 3, body, 0)


def kernel(ctxs, grps, poles, taps, tokens, cotangent, w_ref, inv_ref, gain_ref, skip_ref, out,
           tok_in, cot_in, before, after, cot_after, every,
           natural, cnat, xt, q_at, k_at, v_at, src, ups, dq,
           decay, weights, gain, ends, starts, nexts, begin,
           send_sem, recv_sem, edge_send, edge_recv, state_send, state_recv):
    ctx, grp = lax.axis_index("ctx"), lax.axis_index("grp")
    share, chans = tokens.shape[0], out.shape[1]
    rows = share * grps
    length = rows // SEGS + 1
    chunks = chans // LANES
    first, last = ctx == 0, ctx == ctxs - 1
    lead, tail = grp == 0, grp == grps - 1

    barrier = pltpu.get_barrier_semaphore()

    def greet(to_ctx, to_grp):
        pl.semaphore_signal(barrier, inc=1, device_id=(to_ctx, to_grp), device_id_type=MESH)

    for off in range(1, grps):
        greet(ctx, lax.rem(grp + off, grps))
    for off in range(1, ctxs):
        greet(lax.rem(ctx + off, ctxs), grp)

    @pl.when(ctx > 0)
    def _():
        greet(ctx - 1, grps - 1)

    @pl.when(ctx < ctxs - 1)
    def _():
        greet(ctx + 1, 0)

    sends_tail = jnp.logical_and(tail, ctx < ctxs - 1)
    sends_lead = jnp.logical_and(lead, ctx > 0)
    edges = jnp.where(sends_tail, grps, 0) + jnp.where(sends_lead, grps, 0)
    pl.semaphore_wait(barrier, grps - 1 + ctxs - 1 + edges)

    def edge_copy(kind, j):
        source = (tokens, tokens, cotangent)[kind]
        row = share - HALO if kind == 0 else 0
        return pltpu.make_async_remote_copy(
            src_ref=source.at[row : row + HALO, pl.ds(pl.multiple_of(j * chans, LANES), chans)],
            dst_ref=(before, after, cot_after)[kind],
            send_sem=edge_send.at[kind, j],
            recv_sem=edge_recv.at[kind],
            device_id=(ctx + 1 if kind == 0 else ctx - 1, j),
            device_id_type=MESH,
        )

    @pl.when(sends_tail)
    def _():
        for j in range(grps):
            edge_copy(0, j).start()

    @pl.when(sends_lead)
    def _():
        for j in range(grps):
            edge_copy(1, j).start()
            edge_copy(2, j).start()

    def columns(owner, c):
        return pl.ds(pl.multiple_of(owner * chans + c * LANES, LANES), LANES)

    def block_rows(owner):
        return pl.ds(pl.multiple_of(owner * share, share), share)

    def own_copy(a, c):
        source, target = ((tokens, tok_in), (cotangent, cot_in))[a]
        return pltpu.make_async_copy(
            source.at[:, columns(grp, c)], target.at[c, block_rows(grp), :], recv_sem.at[a, c, grp]
        )

    def block_copy(a, c, sender, receiver):
        source, target = ((tokens, tok_in), (cotangent, cot_in))[a]
        return pltpu.make_async_remote_copy(
            src_ref=source.at[:, columns(receiver, c)],
            dst_ref=target.at[c, block_rows(sender), :],
            send_sem=send_sem.at[a, c, receiver],
            recv_sem=recv_sem.at[a, c, sender],
            device_id=(ctx, receiver),
            device_id_type=MESH,
        )

    def send_blocks(a, c):
        own_copy(a, c).start()
        for off in range(1, grps):
            block_copy(a, c, grp, lax.rem(grp + off, grps)).start()

    def send_next(a, c):
        @pl.when(c + 1 < chunks)
        def _():
            send_blocks(a, c + 1)

    send_blocks(0, 0)
    send_blocks(1, 0)

    @pl.when(first)
    def _():
        before[...] = jnp.zeros_like(before)

    @pl.when(last)
    def _():
        after[...] = jnp.zeros_like(after)
        cot_after[...] = jnp.zeros_like(cot_after)

    @pl.when(ctx > 0)
    def _():
        edge_copy(0, 0).wait_recv()

    @pl.when(ctx < ctxs - 1)
    def _():
        edge_copy(1, 0).wait_recv()
        edge_copy(2, 0).wait_recv()

    def state_copy(kind, c, sender, receiver):
        return pltpu.make_async_remote_copy(
            src_ref=every.at[kind, c, sender],
            dst_ref=every.at[kind, c, sender],
            send_sem=state_send.at[kind, c, receiver],
            recv_sem=state_recv.at[kind, c, sender],
            device_id=(receiver, grp),
            device_id_type=MESH,
        )

    ahead, behind = tuple(range(SEGS)), tuple(reversed(range(SEGS)))

    def here(c):
        return pl.ds(pl.multiple_of(c * LANES, LANES), LANES)

    def arrive(a, c):
        own_copy(a, c).wait()
        for off in range(1, grps):
            sender = lax.rem(grp + off, grps)
            block_copy(a, c, sender, sender).wait_recv()

    def tell(kind, c, total):
        every[kind, c, ctx] = total
        for off in range(1, ctxs):
            state_copy(kind, c, ctx, lax.rem(ctx + off, ctxs)).start()

    def hear(kind, c, inverse):
        for off in range(1, ctxs):
            sender = lax.rem(ctx + off, ctxs)
            state_copy(kind, c, sender, sender).wait_recv()
        over = jnp.exp(-float(rows) * inverse)
        incoming = jnp.zeros_like(inverse)
        for j in range(ctxs):
            if kind == 0:
                incoming = jnp.where(j < ctx, over * incoming + every[0, c, j], incoming)
            else:
                r = ctxs - 1 - j
                incoming = jnp.where(r > ctx, over * incoming + every[1, c, r], incoming)
        return incoming

    def token_phase(c):
        slot, at = lax.rem(c, 2), here(c)
        arrive(0, c)
        send_next(0, c)
        natural[0:HALO, :] = before[:, at].astype(jnp.float32)
        natural[HALO : HALO + rows, :] = tok_in[c].astype(jnp.float32)
        natural[HALO + rows : HALO + rows + HALO, :] = after[:, at].astype(jnp.float32)
        relayout(natural, xt, HALO - (taps - 1), length + taps - 1, length)
        weights[...] = w_ref[:, :, at]
        convolve(length, taps, weights, xt, q_at, k_at.at[slot], v_at.at[slot], src)
        inverse = inv_ref[:, at]
        decay[...] = jnp.exp(-inverse)
        local_states(length, poles, decay, lambda t: src[t], ends)
        tell(0, c, link_segments(length, poles, ahead, inverse, ends, starts))

    def forward_phase(c):
        at = here(c)
        inverse = inv_ref[:, at]
        decay[...] = jnp.exp(-inverse)
        gain[...] = gain_ref[:, at]
        enter(length, poles, ahead, inverse, hear(0, c, inverse), starts, begin)

        def store(t, value):
            dq[t] = value

        mix(length, poles, False, decay, gain, skip_ref[:, at], begin, src, store)

    def cotangent_phase(c):
        at = here(c)
        arrive(1, c)
        send_next(1, c)
        cnat[0:rows, :] = cot_in[c].astype(jnp.float32)
        cnat[rows : rows + HALO, :] = cot_after[:, at].astype(jnp.float32)
        inverse = inv_ref[:, at]
        decay[...] = jnp.exp(-inverse)

        def fetch(step):
            t = length - 1 - step
            value = cnat[pl.ds(t, SEGS, stride=length), :]
            upstream = value * q_at[t]
            ups[t] = upstream
            dq[t] = dq[t] * value
            return upstream

        local_states(length, poles, decay, fetch, ends)
        tell(1, c, link_segments(length, poles, behind, inverse, ends, nexts))

    def gradient_phase(c):
        slot, at = lax.rem(c, 2), here(c)
        weights[...] = w_ref[:, :, at]
        inverse = inv_ref[:, at]
        decay[...] = jnp.exp(-inverse)
        gain[...] = gain_ref[:, at]
        enter(length, poles, behind, inverse, hear(1, c, inverse), nexts, begin)
        k_here, v_here = k_at.at[slot], v_at.at[slot]

        def store(t, value):
            k, v = k_here[t], v_here[t]
            k_here[t] = value * v
            v_here[t] = value * k

        mix(length, poles, True, decay, gain, skip_ref[:, at], begin, ups, store)
        gather_taps(length, taps, weights, (dq, k_here, v_here), natural)
        out[:, at] = natural[0:rows, :].astype(jnp.bfloat16)

    def turn(c, _):
        token_phase(c)

        @pl.when(c > 0)
        def _():
            gradient_phase(c - 1)

        forward_phase(c)
        cotangent_phase(c)
        return 0

    lax.fori_loop(0, chunks, turn, 0)
    gradient_phase(jnp.int32(chunks - 1))

    def drain(c, _):
        for a in range(2):
            for off in range(1, grps):
                block_copy(a, c, grp, lax.rem(grp + off, grps)).wait_send()
            for off in range(1, ctxs):
                state_copy(a, c, ctx, lax.rem(ctx + off, ctxs)).wait_send()
        return 0

    lax.fori_loop(0, chunks, drain, 0)

    @pl.when(sends_tail)
    def _():
        for j in range(grps):
            edge_copy(0, j).wait_send()

    @pl.when(sends_lead)
    def _():
        for j in range(grps):
            edge_copy(1, j).wait_send()
            edge_copy(2, j).wait_send()


def per_device(tokens, cotangent, conv_weight, residue, decay_length, skip_gain):
    ctxs, grps = lax.axis_size("ctx"), lax.axis_size("grp")
    poles, chans = residue.shape
    taps = conv_weight.shape[1]
    rows = tokens.shape[0] * grps
    length = rows // SEGS + 1
    chunks = chans // LANES
    inverse = 1.0 / decay_length
    gain = residue * jnp.sqrt(-jnp.expm1(-2.0 * inverse))
    f32, bf16 = jnp.float32, jnp.bfloat16

    def turned(*lead, extra=0):
        return pltpu.VMEM((*lead, length + extra, SEGS, LANES), f32)

    more = taps - 1
    vmem = pl.BlockSpec(memory_space=pltpu.VMEM)
    far = pl.BlockSpec(memory_space=pl.ANY)
    small = pltpu.VMEM((poles * SEGS, LANES), f32)
    pair = pltpu.VMEM((2, poles * SEGS, LANES), f32)
    linked = pltpu.VMEM((SEGS, poles, LANES), f32)
    edge = pltpu.VMEM((HALO, chans), bf16)
    arrived = pltpu.VMEM((chunks, rows, LANES), bf16)
    natural = pltpu.VMEM((rows + 2 * HALO, LANES), f32)
    dma = pltpu.SemaphoreType.DMA
    return pl.pallas_call(
        functools.partial(kernel, ctxs, grps, poles, taps),
        out_shape=jax.ShapeDtypeStruct((rows, chans), bf16),
        in_specs=[far, far, vmem, vmem, vmem, vmem],
        out_specs=vmem,
        scratch_shapes=[
            arrived, arrived, edge, edge, edge, pltpu.VMEM((2, chunks, ctxs, poles, LANES), f32),
            natural, natural, turned(extra=more), turned(),
            turned(2, extra=more), turned(2, extra=more), turned(), turned(), turned(extra=more),
            pltpu.VMEM((poles, LANES), f32), pltpu.VMEM((3, taps, LANES), f32),
            pltpu.VMEM((poles, LANES), f32), pair, linked, linked, small,
            dma((2, chunks, grps)), dma((2, chunks, grps)), dma((3, grps)), dma((3,)),
            dma((2, chunks, ctxs)), dma((2, chunks, ctxs)),
        ],
        compiler_params=pltpu.CompilerParams(
            vmem_limit_bytes=56 * 2**20, collective_id=0, has_side_effects=True
        ),
    )(tokens, cotangent, conv_weight, inverse, gain, skip_gain[None])


def solution(mesh):
    placed = (
        P(("ctx", "grp"), None),
        P(("ctx", "grp"), None),
        P(None, None, "grp"),
        P(None, "grp"),
        P(None, "grp"),
        P("grp"),
    )
    return jax.shard_map(
        per_device, mesh=mesh, in_specs=placed, out_specs=P("ctx", "grp"), check_vma=False
    )
```
